128 devices in a mesh: dp: 4 (over z), row: 8 (over x, core), col: 4 (over y).
Axes of the slice: x: 4, y: 4, z: 4, core: 2. Of those that a mesh axis runs over, the one named last changes fastest.
Arguments:
- activations: bfloat16 [4096, 6144], P(('dp', 'row'), 'col'), parts along dimension 0, may hold values from -6 to 6
- up_weight: bfloat16 [6144, 24576], P('col', 'row'), may hold values from -0.078125 to 0.078125
- down_weight: bfloat16 [24576, 6144], P(('row', 'col')), may hold values from -0.0625 to 0.0625
Outputs:
- ffn_output: bfloat16 [4096, 6144], P(('dp', 'row', 'col')), parts along dimension 0
The draws below stay inside these ranges and needn't reach their ends.
There are 4 independent parts, one for each index of `dp`. The reference program is written for one: setup_inputs(seed, part) draws one part's arguments, and reference() takes and returns one part's arrays. A program takes and returns all parts, laid end to end along the dimension named above; an argument that names none is the same for every part. Nothing has to cross between parts.
All inputs are finite; a program needn't handle non-finite values.
Results may differ from the reference program's by a relative error of at most 0.027.
Values may be sent and summed in bfloat16 or wider, within the bound.
A program may use at most 128 MiB of HBM per device.

```python
import jax
import jax.numpy as jnp
from jax import lax

D = 6144
FF = 24576
TOKENS = 1024
N_ROW = 8
N_COL = 4


def shard_levels(stream_key, dims, pieces, least, largest):
    gain, own = 1.0, jax.random.fold_in(stream_key, 6)
    for position, shards_of in pieces:
        heights = jnp.exp(jax.random.uniform(jax.random.fold_in(own, position), (shards_of,), jnp.float32, least / len(pieces), largest / len(pieces)))
        gain = gain * jnp.repeat(heights, dims[position] // shards_of).reshape([-1 if axis == position else 1 for axis in range(len(dims))])
    return gain


def normal_values(rng, dims, scale, limit, shards=(), kind=jnp.bfloat16):
    factor_of = shard_levels(rng, dims, shards, -0.22, 0.18) if shards else 1.0
    values = jax.random.normal(rng, dims, jnp.float32) * scale * factor_of
    return jnp.minimum(jnp.maximum(values, -limit), limit).astype(kind)


def setup_inputs(seed: int = 0, part: int = 0) -> dict:
    key_of = jax.random.split(jax.random.key(seed), 4)
    part_keys = jax.random.split(jax.random.fold_in(key_of[3], part), 4)
    activations = normal_values(part_keys[0], (TOKENS, D), 1.0, 6.0, ((0, 8), (1, 4)))
    up_weight = normal_values(key_of[1], (D, FF), D ** -0.5, 0.078125, ((0, 4), (1, 8)))
    down_weight = normal_values(key_of[2], (FF, D), (FF // 3) ** -0.5, 0.0625, ((0, 32),))
    return dict(activations=activations, up_weight=up_weight, down_weight=down_weight)


def tanh_gelu(values):
    inner = 0.7978845608028654 * (values + 0.044715 * values * values * values)
    return 0.5 * values * (1.0 + jnp.tanh(inner))


def rounded(values):
    narrow = lax.optimization_barrier(values.astype(jnp.bfloat16))
    return narrow.astype(jnp.float32)


def reference(activations, up_weight, down_weight):
    feat_block = D // N_COL
    pre_act = jnp.zeros((TOKENS, FF), jnp.float32)
    for block in range(N_COL):
        lo_feat = block * feat_block
        partial_up = jnp.dot(activations[:, lo_feat:lo_feat + feat_block], up_weight[lo_feat:lo_feat + feat_block, :], preferred_element_type=jnp.float32)
        pre_act = pre_act + rounded(partial_up)
    hidden = tanh_gelu(pre_act).astype(jnp.bfloat16)
    hid_block = FF // (N_ROW * N_COL)
    total = jnp.zeros((TOKENS, D), jnp.float32)
    for block in range(N_ROW * N_COL):
        lo_hid = block * hid_block
        term = jnp.dot(hidden[:, lo_hid:lo_hid + hid_block], down_weight[lo_hid:lo_hid + hid_block, :], preferred_element_type=jnp.float32)
        total = total + rounded(term)
    return total.astype(jnp.bfloat16)
```

```python
import functools

import jax
import jax.numpy as jnp
from jax import lax
from jax.experimental import pallas as pl
from jax.experimental.pallas import tpu as pltpu
from jax.sharding import PartitionSpec as P

MESH = pl.DeviceIdType.MESH
F32, BF16 = jnp.float32, jnp.bfloat16
N_X, N_CORE, N_COL = 4, 2, 4
CHUNKS = 8
TILES = 8
UP_SLOTS, DOWN_SLOTS = 3, 2


def tanh_gelu(values):
    inner = 0.7978845608028654 * (values + 0.044715 * values * values * values)
    return 0.5 * values * (1.0 + jnp.tanh(inner))


def wide(ref_value):
    return ref_value.astype(F32)


def kernel(
    act_hbm, up_hbm, down_hbm, out_ref,
    own, act, wu, wd, pu, mid, fin, hid, pd, pr, xm, xf, yt, ys, yr, ot,
    local_sem, wu_sem, wd_sem,
    ag_send, ag_x, ag_p, pu_send, mid_sem, fin_sem, pd_send, pr_sem, x_send, xm_sem, xf_sem, y_send, yr_sem,
):
    dp, row, c = lax.axis_index("dp"), lax.axis_index("row"), lax.axis_index("col")
    x, k = row // N_CORE, row % N_CORE
    rows = act.shape[1] // (N_X * N_CORE)
    half_up = pu.shape[-1]
    tile = wd.shape[-1]
    half = TILES // 2
    group = rows // N_COL

    def device(dx=0, dk=0, dy=0):
        return (dp, lax.rem(x + dx, N_X) * N_CORE + lax.rem(k + dk, N_CORE), lax.rem(c + dy, N_COL))

    right, left, across = device(dx=1), device(dx=3), device(dx=2)
    partner = device(dk=1)
    up_c, down_c, far_c = device(dy=1), device(dy=3), device(dy=2)
    everyone = (right, left, across, partner, up_c, down_c, far_c)

    barrier = pltpu.get_barrier_semaphore()
    for other in everyone:
        pl.semaphore_signal(barrier, inc=1, device_id=other, device_id_type=MESH)

    own_copy = pltpu.make_async_copy(act_hbm, own, local_sem)
    own_copy.start()
    order = (2, 3, 1, 0)

    def wu_copy(g):
        cols = pl.ds(pl.multiple_of(lax.rem(c + order[g], N_COL) * (2 * half_up), 128), 2 * half_up)
        return pltpu.make_async_copy(up_hbm.at[:, cols], wu.at[g], wu_sem.at[g])

    def wd_copy(t):
        return pltpu.make_async_copy(down_hbm.at[:, pl.ds(t * tile, tile)], wd.at[t], wd_sem.at[t])

    for g in range(4):
        wu_copy(g).start()
    for t in range(TILES):
        wd_copy(t).start()

    def send(src, dst, send_sem, recv_sem, to):
        pltpu.make_async_remote_copy(
            src_ref=src, dst_ref=dst, send_sem=send_sem, recv_sem=recv_sem, device_id=to, device_id_type=MESH
        ).start()

    def await_bytes(ref, sem):
        pltpu.make_async_copy(ref, ref, sem).wait()

    def place(core, at_x):
        return pl.ds(pl.multiple_of((core * N_X + at_x) * rows, rows), rows)

    own_copy.wait()
    n_own = rows * CHUNKS
    to_row = lax.broadcasted_iota(jnp.int32, (n_own, n_own), 0)
    from_row = lax.broadcasted_iota(jnp.int32, (n_own, n_own), 1)
    chunk_of, rest = to_row // rows, to_row % rows
    wanted = (rest // group) * (group * CHUNKS) + chunk_of * group + rest % group
    shuffle = jnp.where(from_row == wanted, 1.0, 0.0).astype(BF16)
    shuffled = jnp.dot(shuffle, own[...], preferred_element_type=F32).astype(BF16)
    mine = place(k, x)
    for s in range(CHUNKS):
        act[s, mine, :] = shuffled[s * rows:(s + 1) * rows]

    pl.semaphore_wait(barrier, len(everyone))

    @pl.loop(0, CHUNKS)
    def _(s):
        block = act.at[s, mine]
        send(block, block, ag_send.at[s], ag_x.at[s], right)
        send(block, block, ag_send.at[s], ag_x.at[s], left)
        send(block, block, ag_send.at[s], ag_x.at[s], across)
        send(block, block, ag_send.at[s], ag_p.at[s], partner)

    def forward(s):
        await_bytes(act.at[s, pl.ds(0, 3 * rows)], ag_x.at[s])
        for dx in (1, 3, 2):
            block = act.at[s, place(k, lax.rem(x + dx, N_X))]
            send(block, block, ag_send.at[s], ag_p.at[s], partner)

    def up(s):
        slot = lax.rem(s, UP_SLOTS)

        @pl.when(s >= UP_SLOTS)
        def _():
            await_bytes(pu.at[slot, pl.ds(0, 3)], pu_send.at[slot])

        await_bytes(act.at[s, pl.ds(0, 4 * rows)], ag_p.at[s])
        for g in range(4):
            @pl.when(s == 0)
            def _():
                wu_copy(g).wait()

            part = jnp.dot(act[s], wu[g], preferred_element_type=F32).astype(BF16)
            pu[slot, g, 0] = part[:, :half_up]
            pu[slot, g, 1] = part[:, half_up:]
            if g == 0:
                send(pu.at[slot, 0, 0], mid.at[s, 0], pu_send.at[slot], mid_sem.at[s], down_c)
                send(pu.at[slot, 0, 1], mid.at[s, 1], pu_send.at[slot], mid_sem.at[s], up_c)
            elif g == 1:
                send(pu.at[slot, 1, 1], fin.at[s, 0], pu_send.at[slot], fin_sem.at[s], down_c)
            elif g == 2:
                send(pu.at[slot, 2, 0], fin.at[s, 1], pu_send.at[slot], fin_sem.at[s], up_c)

    def up_mid(s):
        slot = lax.rem(s, UP_SLOTS)
        await_bytes(mid.at[s], mid_sem.at[s])
        pu[slot, 1, 0] = (wide(pu[slot, 1, 0]) + wide(mid[s, 0])).astype(BF16)
        send(pu.at[slot, 1, 0], fin.at[s, 2], pu_send.at[slot], fin_sem.at[s], down_c)
        pu[slot, 2, 1] = (wide(pu[slot, 2, 1]) + wide(mid[s, 1])).astype(BF16)
        send(pu.at[slot, 2, 1], fin.at[s, 3], pu_send.at[slot], fin_sem.at[s], up_c)

    def down(s):
        slot, dslot = lax.rem(s, UP_SLOTS), lax.rem(s, DOWN_SLOTS)
        await_bytes(fin.at[s], fin_sem.at[s])
        first = wide(pu[slot, 3, 0]) + wide(fin[s, 2]) + wide(fin[s, 1])
        hid[:, :half_up] = tanh_gelu(first).astype(BF16)
        second = wide(pu[slot, 3, 1]) + wide(fin[s, 0]) + wide(fin[s, 3])
        hid[:, half_up:] = tanh_gelu(second).astype(BF16)

        @pl.when(s >= DOWN_SLOTS)
        def _():
            await_bytes(pd.at[dslot, 0], pd_send.at[dslot])

        @pl.loop(0, TILES)
        def _(t):
            @pl.when(s == 0)
            def _():
                pltpu.make_async_copy(wd.at[t], wd.at[t], wd_sem.at[t]).wait()

            part = jnp.dot(hid[...], wd[t], preferred_element_type=F32).astype(BF16)
            n = part.shape[0] // 2
            pd[dslot, 0, t] = part[:n]
            pd[dslot, 1, t] = part[n:]
            send(pd.at[dslot, 1 - k, t], pr.at[s, t], pd_send.at[dslot], pr_sem.at[s], partner)

    def rows_of(dx):
        return pl.ds(pl.multiple_of(lax.rem(x + dx, N_X) * rows, rows), rows)

    def pair_sum(s):
        dslot = lax.rem(s, DOWN_SLOTS)
        await_bytes(pr.at[s], pr_sem.at[s])

        @pl.loop(0, TILES)
        def _(t):
            pr[s, t] = (wide(pr[s, t]) + wide(pd[dslot, k, t])).astype(BF16)

        low, high = pl.ds(0, half), pl.ds(half, half)
        send(pr.at[s, low, rows_of(2)], xm.at[s, 0], x_send.at[s], xm_sem.at[s], left)
        send(pr.at[s, high, rows_of(2)], xm.at[s, 1], x_send.at[s], xm_sem.at[s], right)
        send(pr.at[s, high, rows_of(3)], xf.at[s, 0], x_send.at[s], xf_sem.at[s], left)
        send(pr.at[s, low, rows_of(1)], xf.at[s, 1], x_send.at[s], xf_sem.at[s], right)

    def x_mid(s):
        await_bytes(xm.at[s], xm_sem.at[s])
        low, high = pl.ds(0, half), pl.ds(half, half)
        pr[s, low, rows_of(3)] = (wide(pr[s, low, rows_of(3)]) + wide(xm[s, 0])).astype(BF16)
        send(pr.at[s, low, rows_of(3)], xf.at[s, 2], x_send.at[s], xf_sem.at[s], left)
        pr[s, high, rows_of(1)] = (wide(pr[s, high, rows_of(1)]) + wide(xm[s, 1])).astype(BF16)
        send(pr.at[s, high, rows_of(1)], xf.at[s, 3], x_send.at[s], xf_sem.at[s], right)

    def x_end(s):
        await_bytes(xf.at[s], xf_sem.at[s])
        for t in range(TILES):
            total = wide(pr[s, t, rows_of(0)])
            if t < half:
                total = total + wide(xf[s, 2, t]) + wide(xf[s, 1, t])
            else:
                total = total + wide(xf[s, 0, t - half]) + wide(xf[s, 3, t - half])
            q, e = t // 2, t % 2
            for to in range(N_COL):
                yt[to, q * group:(q + 1) * group, e * tile:(e + 1) * tile] = total[to * group:(to + 1) * group]
        for to in range(N_COL):
            ys[s, to] = yt[to].astype(BF16)
        send(ys.at[s, lax.rem(c + 2, N_COL)], yr.at[s, 0], y_send.at[s], yr_sem.at[s], far_c)
        send(ys.at[s, lax.rem(c + 1, N_COL)], yr.at[s, 1], y_send.at[s], yr_sem.at[s], up_c)
        send(ys.at[s, lax.rem(c + 3, N_COL)], yr.at[s, 2], y_send.at[s], yr_sem.at[s], down_c)

    def y_end(s):
        await_bytes(yr.at[s], yr_sem.at[s])
        ot[s] = wide(ys[s, c]) + wide(yr[s, 0]) + wide(yr[s, 1]) + wide(yr[s, 2])

    forward(0)

    @pl.loop(0, CHUNKS + 4)
    def _(i):
        @pl.when((i >= 2) & (i < CHUNKS + 2))
        def _():
            pair_sum(i - 2)

        @pl.when(i < CHUNKS)
        def _():
            up(i)

        @pl.when(i + 1 < CHUNKS)
        def _():
            forward(i + 1)

        @pl.when((i >= 3) & (i < CHUNKS + 3))
        def _():
            x_end(i - 3)

        @pl.when((i >= 1) & (i < CHUNKS + 1))
        def _():
            down(i - 1)

        @pl.when(i < CHUNKS)
        def _():
            up_mid(i)

        @pl.when((i >= 2) & (i < CHUNKS + 2))
        def _():
            x_mid(i - 2)

        @pl.when(i >= 4)
        def _():
            y_end(i - 4)

    wide_cols = ot.shape[-1]
    for s in range(CHUNKS):
        for q in range(N_COL):
            own_out = ot[s, q * group:(q + 1) * group, :]
            yt_rows = slice((s * group) % (4 * group), (s * group) % (4 * group) + group)
            yt[q, yt_rows, :] = own_out
        if s % 4 == 3:
            for q in range(N_COL):
                out_ref[pl.ds((s // 4) * 4 * group, 4 * group), q * wide_cols:(q + 1) * wide_cols] = yt[q].astype(BF16)

    for slot in range(UP_SLOTS):
        await_bytes(pu.at[slot, pl.ds(0, 3)], pu_send.at[slot])
    for slot in range(DOWN_SLOTS):
        await_bytes(pd.at[slot, 0], pd_send.at[slot])

    @pl.loop(0, CHUNKS)
    def _(s):
        await_bytes(act.at[s, pl.ds(0, 7 * rows)], ag_send.at[s])
        await_bytes(pr.at[s, pl.ds(0, 6)], x_send.at[s])
        await_bytes(ys.at[s, pl.ds(0, 3)], y_send.at[s])


def per_device(activations, up_weight, down_weight):
    n_own, depth = activations.shape
    ff_row = up_weight.shape[1]
    ff_own, width = down_weight.shape
    half_up = ff_row // N_COL // 2
    rows = n_own // CHUNKS
    tokens = rows * N_X * N_CORE
    tile = width // TILES
    dma, vmem = pltpu.SemaphoreType.DMA, pltpu.VMEM
    return pl.pallas_call(
        kernel,
        name="fused_feed_forward",
        out_shape=jax.ShapeDtypeStruct((n_own // N_COL, width), BF16),
        in_specs=[pl.BlockSpec(memory_space=pl.ANY)] * 3,
        out_specs=pl.BlockSpec(memory_space=pltpu.VMEM),
        scratch_shapes=[
            vmem((n_own, depth), BF16),
            vmem((CHUNKS, tokens, depth), BF16),
            vmem((4, depth, 2 * half_up), BF16),
            vmem((TILES, ff_own, tile), BF16),
            vmem((UP_SLOTS, 4, 2, tokens, half_up), BF16),
            vmem((CHUNKS, 2, tokens, half_up), BF16),
            vmem((CHUNKS, 4, tokens, half_up), BF16),
            vmem((tokens, ff_own), BF16),
            vmem((DOWN_SLOTS, 2, TILES, tokens // 2, tile), BF16),
            vmem((CHUNKS, TILES, tokens // 2, tile), BF16),
            vmem((CHUNKS, 2, TILES // 2, rows, tile), BF16),
            vmem((CHUNKS, 4, TILES // 2, rows, tile), BF16),
            vmem((N_COL, rows, 2 * tile), F32),
            vmem((CHUNKS, N_COL, rows, 2 * tile), BF16),
            vmem((CHUNKS, 3, rows, 2 * tile), BF16),
            vmem((CHUNKS, rows, 2 * tile), F32),
            dma, dma((4,)), dma((TILES,)),
            dma((CHUNKS,)), dma((CHUNKS,)), dma((CHUNKS,)),
            dma((UP_SLOTS,)), dma((CHUNKS,)), dma((CHUNKS,)),
            dma((DOWN_SLOTS,)), dma((CHUNKS,)),
            dma((CHUNKS,)), dma((CHUNKS,)), dma((CHUNKS,)),
            dma((CHUNKS,)), dma((CHUNKS,)),
        ],
        compiler_params=pltpu.CompilerParams(
            collective_id=0, has_side_effects=True, vmem_limit_bytes=60 * 2**20
        ),
    )(activations, up_weight, down_weight)


def solution(mesh):
    placed = (P(("dp", "row"), "col"), P("col", "row"), P(("row", "col"), None))
    return jax.shard_map(
        per_device,
        mesh=mesh,
        in_specs=placed,
        out_specs=P(("dp", "row", "col"), None),
        check_vma=False,
    )
```

```python
import functools

import jax
import jax.numpy as jnp
from jax import lax
from jax.experimental import pallas as pl
from jax.experimental.pallas import tpu as pltpu
from jax.sharding import PartitionSpec as P

MESH = pl.DeviceIdType.MESH
F32, BF16 = jnp.float32, jnp.bfloat16
N_X, N_CORE, N_COL = 4, 2, 4
CHUNKS = 8
TILES = 8
UP_SLOTS, DOWN_SLOTS = 4, 3
GATHER_DIRECT, RESULT_DIRECT = (0,), (6, 7)
COL_FIRST = ((6, 0), (6, 1))
ORDER = (
    "G0 G1 G2 H0", "F0 H1 H2 G3", "U0 V0 F1 R0", "U1 F2 H3 G4", "A0 G5 G6 V1", "U2 V2 R1 F3",
    "H4 A1 H5 U3", "D0 H6 E0 F4", "V3 P0 G7 A2", "R2 R3 Q0 U4", "D1 E1 Q1 B0", "H7 F5 C0 P1",
    "V4 A3 S1 D2", "E2 C1 U5 P2", "Q2 F6 V5 A4", "S2 R4 D3 F7", "A5 R5 E3 S0", "B2 U6 P3 V6",
    "Q3 D4 R6 C2", "U7 E4 S3 P4", "V7 Q4 D5 C3", "A6 x1 B3 R7", "E5 P5 B1 A7", "x0 Q5 S5 X3",
    "X2 C4 D6 X0", "B5 E6 C5 x2", "x3 P6 S4 z1", "X1 D7 Q6 E7", "S6 B4 X5 Q7", "P7 x5 x4 Z3",
    "S7 C6 Z1 X4", "B6 z3 Z0 z2", "Z5 z0 C7 B7", "z5 Z2 Z4 z4", "x7 x6 Y1 X6", "z7 X7 Z7 Y2",
    "Y3 Z6 Y5 Y4", "z6 Y6 Y0 Y7",
)


def tanh_gelu(values):
    inner = 0.7978845608028654 * (values + 0.044715 * values * values * values)
    return 0.5 * values * (1.0 + jnp.tanh(inner))


def wide(ref_value):
    return ref_value.astype(F32)


def kernel(
    act_hbm, up_hbm, down_hbm, out_ref,
    own, act, wu, wd, pu, mid, fin, hid, pd, pr, xm, xf, yt, ys, ym, yr, ot, ob,
    local_sem, wu_sem, wd_sem,
    ag_send, ag_x, ag_far, ag_p, pu_send, mid_sem, fin_sem, pd_send, pr_sem, x_send, xm_sem, xf_sem, y_send, ym_sem, yr_sem, out_sem,
):
    dp, row, c = lax.axis_index("dp"), lax.axis_index("row"), lax.axis_index("col")
    x, k = row // N_CORE, row % N_CORE
    rows = act.shape[1] // (N_X * N_CORE)
    half_up = pu.shape[-1]
    tile = wd.shape[-1]
    half = TILES // 2
    group = rows // N_COL

    def device(dx=0, dk=0, dy=0):
        return (dp, lax.rem(x + dx, N_X) * N_CORE + lax.rem(k + dk, N_CORE), lax.rem(c + dy, N_COL))

    right, left, across = device(dx=1), device(dx=3), device(dx=2)
    partner = device(dk=1)
    up_c, down_c, far_c = device(dy=1), device(dy=3), device(dy=2)
    everyone = (right, left, across, partner, up_c, down_c, far_c)

    barrier = pltpu.get_barrier_semaphore()
    for other in everyone:
        pl.semaphore_signal(barrier, inc=1, device_id=other, device_id_type=MESH)

    own_copy = pltpu.make_async_copy(act_hbm, own, local_sem)
    own_copy.start()
    order = (2, 3, 1, 0)

    def wu_copy(g):
        cols = pl.ds(pl.multiple_of(lax.rem(c + order[g], N_COL) * (2 * half_up), 128), 2 * half_up)
        return pltpu.make_async_copy(up_hbm.at[:, cols], wu.at[g], wu_sem.at[g])

    def wd_copy(t):
        return pltpu.make_async_copy(down_hbm.at[:, pl.ds(t * tile, tile)], wd.at[t], wd_sem.at[t])

    def send(src, dst, send_sem, recv_sem, to):
        pltpu.make_async_remote_copy(
            src_ref=src, dst_ref=dst, send_sem=send_sem, recv_sem=recv_sem, device_id=to, device_id_type=MESH
        ).start()

    def await_bytes(ref, sem):
        pltpu.make_async_copy(ref, ref, sem).wait()

    def place(core, at_x):
        return pl.ds(pl.multiple_of((core * N_X + at_x) * rows, rows), rows)

    own_copy.wait()
    for g in range(4):
        wu_copy(g).start()
    n_own = rows * CHUNKS
    to_row = lax.broadcasted_iota(jnp.int32, (n_own, n_own), 0)
    from_row = lax.broadcasted_iota(jnp.int32, (n_own, n_own), 1)
    chunk_of, rest = to_row // rows, to_row % rows
    wanted = (rest // group) * (group * CHUNKS) + chunk_of * group + rest % group
    shuffle = jnp.where(from_row == wanted, 1.0, 0.0).astype(BF16)
    shuffled = jnp.dot(shuffle, own[...], preferred_element_type=F32).astype(BF16)
    mine = place(k, x)
    for s in range(CHUNKS):
        act[s, mine, :] = shuffled[s * rows:(s + 1) * rows]

    pl.semaphore_wait(barrier, len(everyone))

    def gather(s):
        block = act.at[s, mine]
        send(block, block, ag_send.at[s], ag_x.at[s], right)
        send(block, block, ag_send.at[s], ag_x.at[s], left)
        if s in GATHER_DIRECT:
            send(block, block, ag_send.at[s], ag_far.at[s], across)
        send(block, block, ag_send.at[s], ag_p.at[s], partner)

    def relay(s):
        await_bytes(act.at[s, pl.ds(0, 2 * rows)], ag_x.at[s])
        from_left, from_right = (act.at[s, place(k, lax.rem(x + dx, N_X))] for dx in (3, 1))
        cut = act.shape[-1] // 2
        if s not in GATHER_DIRECT:
            send(from_left.at[:, :cut], from_left.at[:, :cut], ag_send.at[s], ag_far.at[s], right)
            send(from_right.at[:, cut:], from_right.at[:, cut:], ag_send.at[s], ag_far.at[s], left)
        send(from_left, from_left, ag_send.at[s], ag_p.at[s], partner)
        send(from_right, from_right, ag_send.at[s], ag_p.at[s], partner)

    def forward(s):
        await_bytes(act.at[s, pl.ds(0, rows)], ag_far.at[s])
        block = act.at[s, place(k, lax.rem(x + 2, N_X))]
        send(block, block, ag_send.at[s], ag_p.at[s], partner)

    def up(s):
        slot = s % UP_SLOTS
        if s >= UP_SLOTS:
            await_bytes(pu.at[slot, pl.ds(0, 3)], pu_send.at[slot])

        await_bytes(act.at[s, pl.ds(0, 4 * rows)], ag_p.at[s])
        up_group(s, 0)
        send(pu.at[slot, 0, 0], mid.at[s, 0], pu_send.at[slot], mid_sem.at[s], down_c)
        send(pu.at[slot, 0, 1], mid.at[s, 1], pu_send.at[slot], mid_sem.at[s], up_c)

    def up_group(s, g):
        slot = s % UP_SLOTS
        if s == 0:
            wu_copy(g).wait()
        part = jnp.dot(act[s], wu[g], preferred_element_type=F32).astype(BF16)
        pu[slot, g, 0] = part[:, :half_up]
        pu[slot, g, 1] = part[:, half_up:]

    def up_rest(s):
        for g in range(1, 4):
            up_group(s, g)
        if s == 0:
            for t in range(TILES):
                wd_copy(t).start()

    def up_raws(s):
        slot = s % UP_SLOTS
        send(pu.at[slot, 1, 1], fin.at[s, 0], pu_send.at[slot], fin_sem.at[s], down_c)
        send(pu.at[slot, 2, 0], fin.at[s, 1], pu_send.at[slot], fin_sem.at[s], up_c)

    def up_mid(s):
        slot = s % UP_SLOTS
        await_bytes(mid.at[s], mid_sem.at[s])
        pu[slot, 1, 0] = (wide(pu[slot, 1, 0]) + wide(mid[s, 0])).astype(BF16)
        send(pu.at[slot, 1, 0], fin.at[s, 2], pu_send.at[slot], fin_sem.at[s], down_c)
        pu[slot, 2, 1] = (wide(pu[slot, 2, 1]) + wide(mid[s, 1])).astype(BF16)
        send(pu.at[slot, 2, 1], fin.at[s, 3], pu_send.at[slot], fin_sem.at[s], up_c)

    def gelu(s):
        slot = s % UP_SLOTS
        await_bytes(fin.at[s], fin_sem.at[s])
        first = wide(pu[slot, 3, 0]) + wide(fin[s, 2]) + wide(fin[s, 1])
        hid[:, :half_up] = tanh_gelu(first).astype(BF16)
        second = wide(pu[slot, 3, 1]) + wide(fin[s, 0]) + wide(fin[s, 3])
        hid[:, half_up:] = tanh_gelu(second).astype(BF16)

    def down(s, side):
        dslot = s % DOWN_SLOTS
        if s >= DOWN_SLOTS:
            await_bytes(pd.at[dslot, 0, pl.ds(side * half, half)], pd_send.at[dslot, side])

        @pl.loop(side * half, (side + 1) * half)
        def _(t):
            if s == 0:
                pltpu.make_async_copy(wd.at[t], wd.at[t], wd_sem.at[t]).wait()
            part = jnp.dot(hid[...], wd[t], preferred_element_type=F32).astype(BF16)
            n = part.shape[0] // 2
            pd[dslot, 0, t] = part[:n]
            pd[dslot, 1, t] = part[n:]
            send(pd.at[dslot, 1 - k, t], pr.at[s, t], pd_send.at[dslot, side], pr_sem.at[s, side], partner)

    def swap(s):
        row, col = (lax.broadcasted_iota(jnp.int32, (hid.shape[0],) * 2, axis) for axis in range(2))
        at = row % rows
        source = row // (N_X * rows) * (N_X * rows) + at // group * rows + row // rows % N_X * group + at % group
        select = jnp.where(col == source, 1.0, 0.0).astype(BF16)
        hid[...] = jnp.dot(select, hid[...], preferred_element_type=F32).astype(BF16)

    def down_low(s):
        gelu(s)
        if (s, 0) in COL_FIRST:
            swap(s)
        down(s, 0)

    def down_high(s):
        if ((s, 0) in COL_FIRST) != ((s, 1) in COL_FIRST):
            swap(s)
        down(s, 1)

    def route(s, side):
        along_x, along_y = ((left, right), across, x), ((down_c, up_c), far_c, c)
        return (along_y, along_x) if (s, side) in COL_FIRST else (along_x, along_y)

    def rows_of(at, step):
        return pl.ds(pl.multiple_of(lax.rem(at + step, N_X) * rows, rows), rows)

    low, high = pl.ds(0, half), pl.ds(half, half)
    sides = (low, high)

    def pair_sum(s, side):
        dslot = s % DOWN_SLOTS
        await_bytes(pr.at[s, sides[side]], pr_sem.at[s, side])

        @pl.loop(side * half, (side + 1) * half)
        def _(t):
            pr[s, t] = (wide(pr[s, t]) + wide(pd[dslot, k, t])).astype(BF16)

        near, _, at = route(s, side)[0]
        send(pr.at[s, sides[side], rows_of(at, 2)], xm.at[s, side], x_send.at[s], xm_sem.at[s, side], near[side])

    def pair_low(s):
        pair_sum(s, 0)

    def pair_high(s):
        pair_sum(s, 1)

    def x_raws(s):
        for side in range(2):
            near, _, at = route(s, side)[0]
            where = rows_of(at, 1 + 2 * side)
            send(pr.at[s, sides[side], where], xf.at[s, side, 0], x_send.at[s], xf_sem.at[s, side], near[1 - side])

    def x_mid(s, side):
        await_bytes(xm.at[s, side], xm_sem.at[s, side])
        near, _, at = route(s, side)[0]
        where = rows_of(at, 3 - 2 * side)
        pr[s, sides[side], where] = (wide(pr[s, sides[side], where]) + wide(xm[s, side])).astype(BF16)
        send(pr.at[s, sides[side], where], xf.at[s, side, 1], x_send.at[s], xf_sem.at[s, side], near[side])

    def mid_low(s):
        x_mid(s, 0)

    def mid_high(s):
        x_mid(s, 1)

    cuts = (pl.ds(0, tile), pl.ds(tile, tile))

    def x_end(s, side):
        cut = cuts[side]
        await_bytes(xf.at[s, side], xf_sem.at[s, side])
        for e in range(half):
            total = wide(pr[s, side * half + e, rows_of(route(s, side)[0][2], 0)]) + wide(xf[s, side, 0, e]) + wide(xf[s, side, 1, e])
            for to in range(N_COL):
                yt[to, e * group:(e + 1) * group, :] = total[to * group:(to + 1) * group]
        for to in range(N_COL):
            ys[s, to, :, cut] = yt[to].astype(BF16)
        towards, far, at = route(s, side)[1]
        near, other, opposite = (lax.rem(at + step, N_COL) for step in ((3, 1, 2), (1, 3, 2))[side])
        if s not in RESULT_DIRECT:
            send(ys.at[s, opposite, :, cut], ym.at[s, side], y_send.at[s], ym_sem.at[s, side], towards[side])
        send(ys.at[s, other, :, cut], yr.at[s, 0, :, cut], y_send.at[s], yr_sem.at[s], towards[1 - side])
        if s in RESULT_DIRECT:
            send(ys.at[s, near, :, cut], yr.at[s, 1, :, cut], y_send.at[s], yr_sem.at[s], towards[side])
            send(ys.at[s, opposite, :, cut], yr.at[s, 2, :, cut], y_send.at[s], yr_sem.at[s], far)

    def x_end_low(s):
        x_end(s, 0)

    def x_end_high(s):
        x_end(s, 1)

    def y_mid(s, side):
        if s in RESULT_DIRECT:
            return
        towards, _, at = route(s, side)[1]
        near = lax.rem(at + (3, 1)[side], N_COL)
        cut = cuts[side]
        await_bytes(ym.at[s, side], ym_sem.at[s, side])
        ys[s, near, :, cut] = (wide(ys[s, near, :, cut]) + wide(ym[s, side])).astype(BF16)
        send(ys.at[s, near, :, cut], yr.at[s, 1, :, cut], y_send.at[s], yr_sem.at[s], towards[side])

    def y_mid_low(s):
        y_mid(s, 0)

    def y_mid_high(s):
        y_mid(s, 1)

    per_pass = CHUNKS // 2

    def y_end(s):
        n_parts = 3 if s in RESULT_DIRECT else 2
        await_bytes(yr.at[s, pl.ds(0, n_parts)], yr_sem.at[s])
        total = jnp.concatenate([wide(ys[s, route(s, side)[1][2], :, cuts[side]]) for side in range(2)], axis=1)
        for n in range(n_parts):
            total = total + wide(yr[s, n])
        at = (s % per_pass) * group
        for side in range(2):
            for e in range(half):
                t = side * half + e
                part = total[e * group:(e + 1) * group, side * tile:(side + 1) * tile]
                ot[s // per_pass, at:at + group, t * tile:(t + 1) * tile] = part
        finished.append(s)
        for n in range(2):
            if s // per_pass == n and all(n * per_pass + m in finished for m in range(per_pass)):
                ob[n] = ot[n].astype(BF16)
                out_copy(n).start()

    def out_copy(n):
        block = pl.ds(n * per_pass * group, per_pass * group)
        return pltpu.make_async_copy(ob.at[n], out_ref.at[block], out_sem.at[n])

    finished = []
    stages = {
        "G": gather, "H": relay, "F": forward, "U": up, "V": up_rest, "R": up_raws, "A": up_mid,
        "D": down_low, "E": down_high, "P": pair_low, "Q": pair_high, "S": x_raws, "B": mid_low, "C": mid_high,
        "X": x_end_low, "x": x_end_high, "Z": y_mid_low, "z": y_mid_high, "Y": y_end,
    }
    for line in ORDER:
        for step in line.split():
            stages[step[0]](int(step[1:]))

    for slot in range(UP_SLOTS):
        await_bytes(pu.at[slot, pl.ds(0, 3)], pu_send.at[slot])
    for slot in range(DOWN_SLOTS):
        for side in range(2):
            await_bytes(pd.at[slot, 0, sides[side]], pd_send.at[slot, side])

    @pl.loop(0, CHUNKS)
    def _(s):
        await_bytes(act.at[s, pl.ds(0, 7 * rows)], ag_send.at[s])
        await_bytes(pr.at[s, pl.ds(0, 6)], x_send.at[s])
        await_bytes(ys.at[s, pl.ds(0, 3)], y_send.at[s])

    for n in range(2):
        out_copy(n).wait()


def per_device(activations, up_weight, down_weight):
    n_own, depth = activations.shape
    ff_row = up_weight.shape[1]
    ff_own, width = down_weight.shape
    half_up = ff_row // N_COL // 2
    rows = n_own // CHUNKS
    tokens = rows * N_X * N_CORE
    tile = width // TILES
    dma, vmem = pltpu.SemaphoreType.DMA, pltpu.VMEM
    return pl.pallas_call(
        kernel,
        name="fused_feed_forward",
        out_shape=jax.ShapeDtypeStruct((n_own // N_COL, width), BF16),
        in_specs=[pl.BlockSpec(memory_space=pl.ANY)] * 3,
        out_specs=pl.BlockSpec(memory_space=pl.ANY),
        scratch_shapes=[
            vmem((n_own, depth), BF16),
            vmem((CHUNKS, tokens, depth), BF16),
            vmem((4, depth, 2 * half_up), BF16),
            vmem((TILES, ff_own, tile), BF16),
            vmem((UP_SLOTS, 4, 2, tokens, half_up), BF16),
            vmem((CHUNKS, 2, tokens, half_up), BF16),
            vmem((CHUNKS, 4, tokens, half_up), BF16),
            vmem((tokens, ff_own), BF16),
            vmem((DOWN_SLOTS, 2, TILES, tokens // 2, tile), BF16),
            vmem((CHUNKS, TILES, tokens // 2, tile), BF16),
            vmem((CHUNKS, 2, TILES // 2, rows, tile), BF16),
            vmem((CHUNKS, 2, 2, TILES // 2, rows, tile), BF16),
            vmem((N_COL, rows, tile), F32),
            vmem((CHUNKS, N_COL, rows, 2 * tile), BF16),
            vmem((CHUNKS, 2, rows, tile), BF16),
            vmem((CHUNKS, 3, rows, 2 * tile), BF16),
            vmem((2, rows, width), F32),
            vmem((2, rows, width), BF16),
            dma, dma((4,)), dma((TILES,)),
            dma((CHUNKS,)), dma((CHUNKS,)), dma((CHUNKS,)), dma((CHUNKS,)),
            dma((UP_SLOTS,)), dma((CHUNKS,)), dma((CHUNKS,)),
            dma((DOWN_SLOTS, 2)), dma((CHUNKS, 2)),
            dma((CHUNKS,)), dma((CHUNKS, 2)), dma((CHUNKS, 2)),
            dma((CHUNKS,)), dma((CHUNKS, 2)), dma((CHUNKS,)), dma((2,)),
        ],
        compiler_params=pltpu.CompilerParams(
            collective_id=0, has_side_effects=True, vmem_limit_bytes=60 * 2**20
        ),
    )(activations, up_weight, down_weight)


def solution(mesh):
    placed = (P(("dp", "row"), "col"), P("col", "row"), P(("row", "col"), None))
    return jax.shard_map(
        per_device,
        mesh=mesh,
        in_specs=placed,
        out_specs=P(("dp", "row", "col"), None),
        check_vma=False,
    )
```

```python
import functools

import jax
import jax.numpy as jnp
from jax import lax
from jax.experimental import pallas as pl
from jax.experimental.pallas import tpu as pltpu
from jax.sharding import PartitionSpec as P

MESH = pl.DeviceIdType.MESH
F32, BF16 = jnp.float32, jnp.bfloat16
N_X, N_CORE, N_COL = 4, 2, 4
CHUNKS = 8
TILES = 8
UP_SLOTS, DOWN_SLOTS = 4, 3
GATHER_DIRECT, RESULT_DIRECT = (0,), (6, 7)
COL_FIRST = ((6, 0), (6, 1))
ORDER = (
    "G0 G1 G2 H0", "F0 H1 H2 G3", "U0 V0 F1 R0", "U1 F2 H3 G4", "A0 G5 G6 V1", "U2 V2 R1 F3",
    "H4 A1 H5 U3", "D0 H6 E0 F4", "V3 P0 G7 A2", "R2 R3 Q0 U4", "D1 E1 Q1 B0", "H7 F5 C0 P1",
    "V4 A3 S1 D2", "E2 C1 U5 P2", "Q2 F6 V5 A4", "S2 R4 D3 F7", "A5 R5 E3 S0", "B2 U6 P3 V6",
    "Q3 D4 R6 C2", "U7 E4 S3 P4", "V7 Q4 D5 C3", "A6 x1 B3 R7", "E5 P5 B1 A7", "x0 Q5 S5 X3",
    "X2 C4 D6 X0", "B5 E6 C5 x2", "x3 P6 S4 z1", "X1 D7 Q6 E7", "S6 B4 X5 Q7", "P7 x5 x4 Z3",
    "S7 C6 Z1 X4", "B6 z3 Z0 z2", "Z5 z0 C7 B7", "z5 Z2 Z4 z4", "x7 x6 Y1 X6", "z7 X7 Z7 Y2",
    "Y3 Z6 Y5 Y4", "z6 Y6 Y0 Y7",
)


def tanh_gelu(values):
    inner = 0.7978845608028654 * (values + 0.044715 * values * values * values)
    return 0.5 * values * (1.0 + jnp.tanh(inner))


def wide(ref_value):
    return ref_value.astype(F32)


def kernel(
    act_hbm, up_hbm, down_hbm, out_ref,
    own, act, wu, wd, pu, mid, fin, hid, pd, pr, xm, xf, yt, ys, ym, yr, ot, ob,
    local_sem, wu_sem, wd_sem,
    ag_send, ag_x, ag_far, ag_p, pu_send, mid_sem, fin_sem, pd_send, pr_sem, x_send, xm_sem, xf_sem, y_send, ym_sem, yr_sem, out_sem,
):
    dp, row, c = lax.axis_index("dp"), lax.axis_index("row"), lax.axis_index("col")
    x, k = row // N_CORE, row % N_CORE
    rows = act.shape[1] // (N_X * N_CORE)
    half_up = pu.shape[-1]
    tile = wd.shape[-1]
    half = TILES // 2
    group = rows // N_COL

    def device(dx=0, dk=0, dy=0):
        return (dp, lax.rem(x + dx, N_X) * N_CORE + lax.rem(k + dk, N_CORE), lax.rem(c + dy, N_COL))

    right, left, across = device(dx=1), device(dx=3), device(dx=2)
    partner = device(dk=1)
    up_c, down_c, far_c = device(dy=1), device(dy=3), device(dy=2)
    everyone = (right, left, across, partner, up_c, down_c, far_c)

    barrier = pltpu.get_barrier_semaphore()
    for other in everyone:
        pl.semaphore_signal(barrier, inc=1, device_id=other, device_id_type=MESH)

    own_copy = pltpu.make_async_copy(act_hbm, own, local_sem)
    own_copy.start()
    order = (2, 3, 1, 0)

    def wu_copy(g):
        cols = pl.ds(pl.multiple_of(lax.rem(c + order[g], N_COL) * (2 * half_up), 128), 2 * half_up)
        return pltpu.make_async_copy(up_hbm.at[:, cols], wu.at[g], wu_sem.at[g])

    def wd_copy(t):
        return pltpu.make_async_copy(down_hbm.at[:, pl.ds(t * tile, tile)], wd.at[t], wd_sem.at[t])

    def send(src, dst, send_sem, recv_sem, to):
        pltpu.make_async_remote_copy(
            src_ref=src, dst_ref=dst, send_sem=send_sem, recv_sem=recv_sem, device_id=to, device_id_type=MESH
        ).start()

    def await_bytes(ref, sem):
        pltpu.make_async_copy(ref, ref, sem).wait()

    def place(core, at_x):
        return pl.ds(pl.multiple_of((core * N_X + at_x) * rows, rows), rows)

    own_copy.wait()
    for g in range(4):
        wu_copy(g).start()
    n_own = rows * CHUNKS
    to_row = lax.broadcasted_iota(jnp.int32, (n_own, n_own), 0)
    from_row = lax.broadcasted_iota(jnp.int32, (n_own, n_own), 1)
    chunk_of, rest = to_row // rows, to_row % rows
    wanted = (rest // group) * (group * CHUNKS) + chunk_of * group + rest % group
    shuffle = jnp.where(from_row == wanted, 1.0, 0.0).astype(BF16)
    shuffled = jnp.dot(shuffle, own[...], preferred_element_type=F32).astype(BF16)
    mine = place(k, x)
    for s in range(CHUNKS):
        act[s, mine, :] = shuffled[s * rows:(s + 1) * rows]

    pl.semaphore_wait(barrier, len(everyone))

    def gather(s):
        block = act.at[s, mine]
        if s in GATHER_DIRECT:
            send(block, block, ag_send.at[s], ag_far.at[s], across)
        send(block, block, ag_send.at[s], ag_x.at[s], right)
        send(block, block, ag_send.at[s], ag_x.at[s], left)
        send(block, block, ag_send.at[s], ag_p.at[s], partner)

    def relay(s):
        await_bytes(act.at[s, pl.ds(0, 2 * rows)], ag_x.at[s])
        from_left, from_right = (act.at[s, place(k, lax.rem(x + dx, N_X))] for dx in (3, 1))
        cut = act.shape[-1] // 2
        if s not in GATHER_DIRECT:
            send(from_left.at[:, :cut], from_left.at[:, :cut], ag_send.at[s], ag_far.at[s], right)
            send(from_right.at[:, cut:], from_right.at[:, cut:], ag_send.at[s], ag_far.at[s], left)
        send(from_left, from_left, ag_send.at[s], ag_p.at[s], partner)
        send(from_right, from_right, ag_send.at[s], ag_p.at[s], partner)

    def forward(s):
        await_bytes(act.at[s, pl.ds(0, rows)], ag_far.at[s])
        block = act.at[s, place(k, lax.rem(x + 2, N_X))]
        send(block, block, ag_send.at[s], ag_p.at[s], partner)

    def up(s):
        slot = s % UP_SLOTS
        if s >= UP_SLOTS:
            await_bytes(pu.at[slot, pl.ds(0, 3)], pu_send.at[slot])

        await_bytes(act.at[s, pl.ds(0, 4 * rows)], ag_p.at[s])
        up_group(s, 0)
        send(pu.at[slot, 0, 0], mid.at[s, 0], pu_send.at[slot], mid_sem.at[s], down_c)
        send(pu.at[slot, 0, 1], mid.at[s, 1], pu_send.at[slot], mid_sem.at[s], up_c)

    def up_group(s, g):
        slot = s % UP_SLOTS
        if s == 0:
            wu_copy(g).wait()
        part = jnp.dot(act[s], wu[g], preferred_element_type=F32).astype(BF16)
        pu[slot, g, 0] = part[:, :half_up]
        pu[slot, g, 1] = part[:, half_up:]

    def up_rest(s):
        for g in range(1, 4):
            up_group(s, g)
        if s == 0:
            for t in range(TILES):
                wd_copy(t).start()

    def up_raws(s):
        slot = s % UP_SLOTS
        send(pu.at[slot, 1, 1], fin.at[s, 0], pu_send.at[slot], fin_sem.at[s], down_c)
        send(pu.at[slot, 2, 0], fin.at[s, 1], pu_send.at[slot], fin_sem.at[s], up_c)

    def up_mid(s):
        slot = s % UP_SLOTS
        await_bytes(mid.at[s], mid_sem.at[s])
        pu[slot, 1, 0] = (wide(pu[slot, 1, 0]) + wide(mid[s, 0])).astype(BF16)
        send(pu.at[slot, 1, 0], fin.at[s, 2], pu_send.at[slot], fin_sem.at[s], down_c)
        pu[slot, 2, 1] = (wide(pu[slot, 2, 1]) + wide(mid[s, 1])).astype(BF16)
        send(pu.at[slot, 2, 1], fin.at[s, 3], pu_send.at[slot], fin_sem.at[s], up_c)

    def gelu(s):
        slot = s % UP_SLOTS
        await_bytes(fin.at[s], fin_sem.at[s])
        first = wide(pu[slot, 3, 0]) + wide(fin[s, 2]) + wide(fin[s, 1])
        hid[:, :half_up] = tanh_gelu(first).astype(BF16)
        second = wide(pu[slot, 3, 1]) + wide(fin[s, 0]) + wide(fin[s, 3])
        hid[:, half_up:] = tanh_gelu(second).astype(BF16)

    def down(s, side):
        dslot = s % DOWN_SLOTS
        if s >= DOWN_SLOTS:
            await_bytes(pd.at[dslot, 0, pl.ds(side * half, half)], pd_send.at[dslot, side])

        @pl.loop(side * half, (side + 1) * half)
        def _(t):
            if s == 0:
                pltpu.make_async_copy(wd.at[t], wd.at[t], wd_sem.at[t]).wait()
            part = jnp.dot(hid[...], wd[t], preferred_element_type=F32).astype(BF16)
            n = part.shape[0] // 2
            pd[dslot, 0, t] = part[:n]
            pd[dslot, 1, t] = part[n:]
            send(pd.at[dslot, 1 - k, t], pr.at[s, t], pd_send.at[dslot, side], pr_sem.at[s, side], partner)

    def swap(s):
        row, col = (lax.broadcasted_iota(jnp.int32, (hid.shape[0],) * 2, axis) for axis in range(2))
        at = row % rows
        source = row // (N_X * rows) * (N_X * rows) + at // group * rows + row // rows % N_X * group + at % group
        select = jnp.where(col == source, 1.0, 0.0).astype(BF16)
        hid[...] = jnp.dot(select, hid[...], preferred_element_type=F32).astype(BF16)

    def down_low(s):
        gelu(s)
        if (s, 0) in COL_FIRST:
            swap(s)
        down(s, 0)

    def down_high(s):
        if ((s, 0) in COL_FIRST) != ((s, 1) in COL_FIRST):
            swap(s)
        down(s, 1)

    def route(s, side):
        along_x, along_y = ((left, right), across, x), ((down_c, up_c), far_c, c)
        return (along_y, along_x) if (s, side) in COL_FIRST else (along_x, along_y)

    def rows_of(at, step):
        return pl.ds(pl.multiple_of(lax.rem(at + step, N_X) * rows, rows), rows)

    low, high = pl.ds(0, half), pl.ds(half, half)
    sides = (low, high)

    def pair_sum(s, side):
        dslot = s % DOWN_SLOTS
        await_bytes(pr.at[s, sides[side]], pr_sem.at[s, side])

        @pl.loop(side * half, (side + 1) * half)
        def _(t):
            pr[s, t] = (wide(pr[s, t]) + wide(pd[dslot, k, t])).astype(BF16)

        near, _, at = route(s, side)[0]
        send(pr.at[s, sides[side], rows_of(at, 2)], xm.at[s, side], x_send.at[s], xm_sem.at[s, side], near[side])

    def pair_low(s):
        pair_sum(s, 0)

    def pair_high(s):
        pair_sum(s, 1)

    def x_raws(s):
        for side in range(2):
            near, _, at = route(s, side)[0]
            where = rows_of(at, 1 + 2 * side)
            send(pr.at[s, sides[side], where], xf.at[s, side, 0], x_send.at[s], xf_sem.at[s, side], near[1 - side])

    def x_mid(s, side):
        await_bytes(xm.at[s, side], xm_sem.at[s, side])
        near, _, at = route(s, side)[0]
        where = rows_of(at, 3 - 2 * side)
        pr[s, sides[side], where] = (wide(pr[s, sides[side], where]) + wide(xm[s, side])).astype(BF16)
        send(pr.at[s, sides[side], where], xf.at[s, side, 1], x_send.at[s], xf_sem.at[s, side], near[side])

    def mid_low(s):
        x_mid(s, 0)

    def mid_high(s):
        x_mid(s, 1)

    cuts = (pl.ds(0, tile), pl.ds(tile, tile))

    def x_end(s, side):
        cut = cuts[side]
        await_bytes(xf.at[s, side], xf_sem.at[s, side])
        for e in range(half):
            total = wide(pr[s, side * half + e, rows_of(route(s, side)[0][2], 0)]) + wide(xf[s, side, 0, e]) + wide(xf[s, side, 1, e])
            for to in range(N_COL):
                yt[to, e * group:(e + 1) * group, :] = total[to * group:(to + 1) * group]
        for to in range(N_COL):
            ys[s, to, :, cut] = yt[to].astype(BF16)
        towards, far, at = route(s, side)[1]
        near, other, opposite = (lax.rem(at + step, N_COL) for step in ((3, 1, 2), (1, 3, 2))[side])
        if s in RESULT_DIRECT:
            send(ys.at[s, opposite, :, cut], yr.at[s, 2, :, cut], y_send.at[s], yr_sem.at[s], far)
        else:
            send(ys.at[s, opposite, :, cut], ym.at[s, side], y_send.at[s], ym_sem.at[s, side], towards[side])
        send(ys.at[s, other, :, cut], yr.at[s, 0, :, cut], y_send.at[s], yr_sem.at[s], towards[1 - side])
        if s in RESULT_DIRECT:
            send(ys.at[s, near, :, cut], yr.at[s, 1, :, cut], y_send.at[s], yr_sem.at[s], towards[side])

    def x_end_low(s):
        x_end(s, 0)

    def x_end_high(s):
        x_end(s, 1)

    def y_mid(s, side):
        if s in RESULT_DIRECT:
            return
        towards, _, at = route(s, side)[1]
        near = lax.rem(at + (3, 1)[side], N_COL)
        cut = cuts[side]
        await_bytes(ym.at[s, side], ym_sem.at[s, side])
        ys[s, near, :, cut] = (wide(ys[s, near, :, cut]) + wide(ym[s, side])).astype(BF16)
        send(ys.at[s, near, :, cut], yr.at[s, 1, :, cut], y_send.at[s], yr_sem.at[s], towards[side])

    def y_mid_low(s):
        y_mid(s, 0)

    def y_mid_high(s):
        y_mid(s, 1)

    per_pass = CHUNKS // 2

    def y_end(s):
        n_parts = 3 if s in RESULT_DIRECT else 2
        await_bytes(yr.at[s, pl.ds(0, n_parts)], yr_sem.at[s])
        total = jnp.concatenate([wide(ys[s, route(s, side)[1][2], :, cuts[side]]) for side in range(2)], axis=1)
        for n in range(n_parts):
            total = total + wide(yr[s, n])
        at = (s % per_pass) * group
        for side in range(2):
            for e in range(half):
                t = side * half + e
                part = total[e * group:(e + 1) * group, side * tile:(side + 1) * tile]
                ot[s // per_pass, at:at + group, t * tile:(t + 1) * tile] = part
        finished.append(s)
        for n in range(2):
            if s // per_pass == n and all(n * per_pass + m in finished for m in range(per_pass)):
                ob[n] = ot[n].astype(BF16)
                out_copy(n).start()

    def out_copy(n):
        block = pl.ds(n * per_pass * group, per_pass * group)
        return pltpu.make_async_copy(ob.at[n], out_ref.at[block], out_sem.at[n])

    finished = []
    stages = {
        "G": gather, "H": relay, "F": forward, "U": up, "V": up_rest, "R": up_raws, "A": up_mid,
        "D": down_low, "E": down_high, "P": pair_low, "Q": pair_high, "S": x_raws, "B": mid_low, "C": mid_high,
        "X": x_end_low, "x": x_end_high, "Z": y_mid_low, "z": y_mid_high, "Y": y_end,
    }
    for line in ORDER:
        for step in line.split():
            stages[step[0]](int(step[1:]))

    for slot in range(UP_SLOTS):
        await_bytes(pu.at[slot, pl.ds(0, 3)], pu_send.at[slot])
    for slot in range(DOWN_SLOTS):
        for side in range(2):
            await_bytes(pd.at[slot, 0, sides[side]], pd_send.at[slot, side])

    @pl.loop(0, CHUNKS)
    def _(s):
        await_bytes(act.at[s, pl.ds(0, 7 * rows)], ag_send.at[s])
        await_bytes(pr.at[s, pl.ds(0, 6)], x_send.at[s])
        await_bytes(ys.at[s, pl.ds(0, 3)], y_send.at[s])

    for n in range(2):
        out_copy(n).wait()


def per_device(activations, up_weight, down_weight):
    n_own, depth = activations.shape
    ff_row = up_weight.shape[1]
    ff_own, width = down_weight.shape
    half_up = ff_row // N_COL // 2
    rows = n_own // CHUNKS
    tokens = rows * N_X * N_CORE
    tile = width // TILES
    dma, vmem = pltpu.SemaphoreType.DMA, pltpu.VMEM
    return pl.pallas_call(
        kernel,
        name="fused_feed_forward",
        out_shape=jax.ShapeDtypeStruct((n_own // N_COL, width), BF16),
        in_specs=[pl.BlockSpec(memory_space=pl.ANY)] * 3,
        out_specs=pl.BlockSpec(memory_space=pl.ANY),
        scratch_shapes=[
            vmem((n_own, depth), BF16),
            vmem((CHUNKS, tokens, depth), BF16),
            vmem((4, depth, 2 * half_up), BF16),
            vmem((TILES, ff_own, tile), BF16),
            vmem((UP_SLOTS, 4, 2, tokens, half_up), BF16),
            vmem((CHUNKS, 2, tokens, half_up), BF16),
            vmem((CHUNKS, 4, tokens, half_up), BF16),
            vmem((tokens, ff_own), BF16),
            vmem((DOWN_SLOTS, 2, TILES, tokens // 2, tile), BF16),
            vmem((CHUNKS, TILES, tokens // 2, tile), BF16),
            vmem((CHUNKS, 2, TILES // 2, rows, tile), BF16),
            vmem((CHUNKS, 2, 2, TILES // 2, rows, tile), BF16),
            vmem((N_COL, rows, tile), F32),
            vmem((CHUNKS, N_COL, rows, 2 * tile), BF16),
            vmem((CHUNKS, 2, rows, tile), BF16),
            vmem((CHUNKS, 3, rows, 2 * tile), BF16),
            vmem((2, rows, width), F32),
            vmem((2, rows, width), BF16),
            dma, dma((4,)), dma((TILES,)),
            dma((CHUNKS,)), dma((CHUNKS,)), dma((CHUNKS,)), dma((CHUNKS,)),
            dma((UP_SLOTS,)), dma((CHUNKS,)), dma((CHUNKS,)),
            dma((DOWN_SLOTS, 2)), dma((CHUNKS, 2)),
            dma((CHUNKS,)), dma((CHUNKS, 2)), dma((CHUNKS, 2)),
            dma((CHUNKS,)), dma((CHUNKS, 2)), dma((CHUNKS,)), dma((2,)),
        ],
        compiler_params=pltpu.CompilerParams(
            collective_id=0, has_side_effects=True, vmem_limit_bytes=60 * 2**20
        ),
    )(activations, up_weight, down_weight)


def solution(mesh):
    placed = (P(("dp", "row"), "col"), P("col", "row"), P(("row", "col"), None))
    return jax.shard_map(
        per_device,
        mesh=mesh,
        in_specs=placed,
        out_specs=P(("dp", "row", "col"), None),
        check_vma=False,
    )
```
